32 devices in a mesh: row: 8 (over z, x), col: 4 (over y, core).
Axes of the slice: x: 2, y: 2, z: 4, core: 2. Of those that a mesh axis runs over, the one named last changes fastest.
Arguments:
- state: float32 [3, 64, 64, 512], P(None, None, 'row', 'col'), may hold values from -1.5 to 3, as said below
- gauge_cells: int32 [8, 4, 2, 32], P('row', 'col'), may hold values from 0 to 1023
- gauge_count: int32 [8, 4, 2], P('row', 'col'), may hold values from 0 to 32, as said below
- obs_value: float32 [8, 4, 2, 32], P('row', 'col'), may hold values from 0.5 to 3
- obs_noise: float32 [8, 4, 2, 32, 64], P('row', 'col'), may hold values from -1.5 to 1.5
- obs_var: float32 [8, 4, 2, 32], P('row', 'col'), may hold values from 0.02 to 0.5
Outputs:
- analysis: float32 [3, 64, 64, 512], P(None, None, 'row', 'col')
The draws below stay inside these ranges and needn't reach their ends.
Inputs may be any that keep to these rules, and one draw needn't show every extreme that they name: `state`: field 0 is depth, from 0.5 to 3.0; fields 1 and 2 are momenta, from -1.5 to 1.5. `gauge_count`: at most 32 live slots; in every batch some tile has all 32 slots live.
All inputs are finite; a program needn't handle non-finite values.
Results may differ from the reference program's by a relative error of at most 0.0003.
Values sent between devices are 32-bit elements; how exact they have to be, the bound alone decides.
A program may use at most 64 MiB of HBM per device.

```python
import math
import jax
import jax.numpy as jnp
from jax import lax

ENSEMBLE_SIZE = 64
TILE_ROWS_SIZE = 8
TILE_COLUMNS = 128
GT = 32
BATCHES = 2
LOC = 6
GRID_ROWS = 64
GRID_COLUMNS = 512
N_ROW = 8
N_COL = 4


def draw_state(key, part):
    k_depth, k_flow = jax.random.split(jax.random.fold_in(key, 11))
    grid_depth = (1, ENSEMBLE_SIZE, GRID_ROWS, GRID_COLUMNS)
    grid_flow = (2, ENSEMBLE_SIZE, GRID_ROWS, GRID_COLUMNS)
    water_depth = 0.5 + 2.5 * jax.random.uniform(k_depth, grid_depth, jnp.float32)
    momentum = jnp.clip(0.3 * jax.random.normal(k_flow, grid_flow, jnp.float32), -1.5, 1.5)
    return jnp.concatenate([water_depth, momentum], axis=0)


def draw_gauge_count(key, part):
    k_dense, k_light, k_heavy, k_full = jax.random.split(jax.random.fold_in(key, 23), 4)
    grid_shape = (N_ROW, N_COL, BATCHES)
    dense_tile = jax.random.randint(k_dense, grid_shape, 0, 8) == 0
    light_count = jax.random.randint(k_light, grid_shape, 0, GT // 4 + 1)
    heavy_count = jax.random.randint(k_heavy, grid_shape, GT // 2, GT + 1)
    counts = jnp.where(dense_tile, heavy_count, light_count)
    full_tile = jax.random.randint(k_full, (BATCHES,), 0, N_ROW * N_COL)
    tile_number = jnp.arange(N_ROW * N_COL, dtype=jnp.int32).reshape(N_ROW, N_COL, 1)
    counts = jnp.where(tile_number == full_tile[None, None, :], GT, counts)
    return counts.astype(jnp.int32)


def plant(values, own_key, low, top_value):
    extent = values.shape
    index_at = [jax.random.randint(jax.random.fold_in(own_key, axis), (), 0, extent[axis]) for axis in range(len(extent))]
    values = values.at[tuple(index_at)].set(low)
    longest = extent.index(max(extent))
    index_at[longest] = (index_at[longest] + 1) % extent[longest]
    return values.at[tuple(index_at)].set(top_value)


def block_levels(rng, dims, cuts, low, top_value):
    def one(position, shards_of):
        heights = jax.random.uniform(jax.random.fold_in(jax.random.fold_in(rng, 6), position), (shards_of,), jnp.float32, low / len(cuts), top_value / len(cuts))
        return jnp.repeat(jnp.exp(heights), dims[position] // shards_of).reshape((-1,) + (1,) * (len(dims) - position - 1))

    gain = one(*cuts[0])
    for cut in cuts[1:]:
        gain = gain * one(*cut)
    return gain


def centred(rng, extent, width, most, cuts=(), kind=jnp.bfloat16):
    gain = block_levels(rng, extent, cuts, -0.22, 0.18) if cuts else 1.0
    drawn = jax.random.normal(rng, extent, jnp.float32) * width * gain
    return jnp.minimum(jnp.maximum(drawn, -most), most).astype(kind)


def setup_inputs(seed: int = 0) -> dict:
    key_list = jax.random.split(jax.random.key(seed), 7)
    return {
        "state": draw_state(jax.random.fold_in(key_list[6], 71), 0),
        "gauge_cells": plant(jax.random.randint(key_list[1], (N_ROW, N_COL, BATCHES, GT), 0, TILE_ROWS_SIZE * TILE_COLUMNS), jax.random.fold_in(key_list[1], 1), 0, (TILE_ROWS_SIZE * TILE_COLUMNS) - 1).astype(jnp.int32),
        "gauge_count": draw_gauge_count(jax.random.fold_in(key_list[6], 71), 0),
        "obs_value": jnp.clip(0.5 + 2.5 * jax.random.uniform(key_list[3], (N_ROW, N_COL, BATCHES, GT), jnp.float32) ** block_levels(key_list[3], (N_ROW, N_COL, BATCHES, GT), ((0, 8), (1, 4)), -0.2, 0.2), 0.5, 3.0),
        "obs_noise": centred(key_list[4], (N_ROW, N_COL, BATCHES, GT, ENSEMBLE_SIZE), 0.3, 1.5, ((0, 8), (1, 4)), jnp.float32),
        "obs_var": jnp.clip(jnp.exp(math.log(0.5) - 3.218876 * jax.random.uniform(key_list[5], (N_ROW, N_COL, BATCHES, GT), jnp.float32) ** block_levels(key_list[5], (N_ROW, N_COL, BATCHES, GT), ((0, 8), (1, 4)), -0.2, 0.2)), 0.02, 0.5),
    }


gravity = 9.81
spacing = 2.0
timestep_length = 0.08

def unit_vector(normal_axis, rank_count):
    entries = [0.0, 1.0, 0.0] if normal_axis == 1 else [0.0, 0.0, 1.0]
    return jnp.array(entries, jnp.float32).reshape((3,) + (1,) * (rank_count - 1))

def physical_flux(values, normal_axis):
    water_depth = values[0]
    normal_vel = values[normal_axis] / water_depth
    pressure = 0.5 * gravity * water_depth * water_depth
    return values * normal_vel[None] + pressure[None] * unit_vector(normal_axis, values.ndim)

def hll_flux(lower, upper, normal_axis):
    speed_l = jnp.sqrt(gravity * lower[0])
    speed_r = jnp.sqrt(gravity * upper[0])
    vel_l = lower[normal_axis] / lower[0]
    vel_r = upper[normal_axis] / upper[0]
    slow_wave = jnp.minimum(jnp.minimum(vel_l - speed_l, vel_r - speed_r), 0.0)
    fast_wave = jnp.maximum(jnp.maximum(vel_l + speed_l, vel_r + speed_r), 0.0)
    numer = fast_wave[None] * physical_flux(lower, normal_axis) - slow_wave[None] * physical_flux(upper, normal_axis)
    numer = numer + (slow_wave * fast_wave)[None] * (upper - lower)
    return numer / (fast_wave - slow_wave)[None]

def state_tendency(padded):
    flux_c = hll_flux(padded[..., 1:-1, :-1], padded[..., 1:-1, 1:], 1)
    flux_r = hll_flux(padded[..., :-1, 1:-1], padded[..., 1:, 1:-1], 2)
    return -(flux_c[..., 1:] - flux_c[..., :-1] + flux_r[..., 1:, :] - flux_r[..., :-1, :]) / spacing

def walls(padded, rim_width, at_top, at_bottom, at_left, at_right):
    rank_count = padded.ndim
    sign_rows = jnp.array([1.0, 1.0, -1.0], jnp.float32).reshape((3,) + (1,) * (rank_count - 1))
    sign_cols = jnp.array([1.0, -1.0, 1.0], jnp.float32).reshape((3,) + (1,) * (rank_count - 1))
    mirror_top = jnp.flip(padded[..., rim_width:2 * rim_width, :], axis=-2) * sign_rows
    padded = padded.at[..., :rim_width, :].set(jnp.where(at_top, mirror_top, padded[..., :rim_width, :]))
    mirror_bottom = jnp.flip(padded[..., -2 * rim_width:-rim_width, :], axis=-2) * sign_rows
    padded = padded.at[..., -rim_width:, :].set(jnp.where(at_bottom, mirror_bottom, padded[..., -rim_width:, :]))
    mirror_left = jnp.flip(padded[..., rim_width:2 * rim_width], axis=-1) * sign_cols
    padded = padded.at[..., :rim_width].set(jnp.where(at_left, mirror_left, padded[..., :rim_width]))
    mirror_right = jnp.flip(padded[..., -2 * rim_width:-rim_width], axis=-1) * sign_cols
    padded = padded.at[..., -rim_width:].set(jnp.where(at_right, mirror_right, padded[..., -rim_width:]))
    return padded

def pack(prior_observation, slot_cells, live_count, obs_value, obs_noise, obs_var, tile_row, tile_col, tile_row_count, tile_column_count):
    member_states = prior_observation.shape[-1]
    slots = prior_observation.shape[-2]
    obs_anom = prior_observation - lax.optimization_barrier(jnp.mean(prior_observation, axis=-1, keepdims=True))
    spread = lax.optimization_barrier(jnp.sum(obs_anom * obs_anom, axis=-1)) / (member_states - 1)
    live_mask = (jnp.arange(slots, dtype=jnp.int32) < live_count[..., None]).astype(jnp.float32)
    obs_weight = live_mask[..., None] * (obs_value[..., None] + obs_noise - prior_observation) / (spread + obs_var)[..., None]
    gauge_grid_row = tile_row * tile_row_count + slot_cells // tile_column_count
    gauge_column = tile_col * tile_column_count + slot_cells % tile_column_count
    coords = jnp.stack([gauge_grid_row, gauge_column], axis=-1).astype(jnp.float32)
    return (obs_anom, obs_weight, coords)

def increments(fields, cell_rows, cell_cols, obs_anom, obs_weight, coords):
    member_states = fields.shape[1]
    centered = fields - lax.optimization_barrier(jnp.mean(fields, axis=1, keepdims=True))
    covariance = jnp.einsum('fmp,gm->fpg', centered, obs_anom, precision=lax.Precision.HIGHEST) / (member_states - 1)
    distance_sq = (cell_rows[:, None] - coords[None, :, 0]) ** 2 + (cell_cols[:, None] - coords[None, :, 1]) ** 2
    taper_weight = jnp.maximum(1.0 - distance_sq / (LOC * LOC), 0.0) ** 2
    return jnp.einsum('fpg,gm->fmp', covariance * taper_weight[None], obs_weight, precision=lax.Precision.HIGHEST)

def march_forward(member_state):
    ghosted = walls(jnp.pad(member_state, ((0, 0), (1, 1), (1, 1))), 1, True, True, True, True)
    opening_section = member_state + timestep_length * state_tendency(ghosted)
    ghosted = walls(jnp.pad(opening_section, ((0, 0), (1, 1), (1, 1))), 1, True, True, True, True)
    return 0.5 * (member_state + opening_section + timestep_length * state_tendency(ghosted))

def reference(state, gauge_cells, gauge_count, obs_value, obs_noise, obs_var):
    predict_flood = jnp.moveaxis(lax.map(march_forward, jnp.moveaxis(state, 1, 0)), 0, 1)
    tile_row = jnp.arange(N_ROW, dtype=jnp.int32)[:, None, None]
    tile_col = jnp.arange(N_COL, dtype=jnp.int32)[None, :, None]
    zero_index = jnp.zeros((), jnp.int32)
    for batch in range(BATCHES):
        slot_cells = gauge_cells[:, :, batch, :]
        gauge_grid_row = tile_row * TILE_ROWS_SIZE + slot_cells // TILE_COLUMNS
        gauge_column = tile_col * TILE_COLUMNS + slot_cells % TILE_COLUMNS
        prior_observation = jnp.moveaxis(predict_flood[0][:, gauge_grid_row, gauge_column], 0, -1)
        obs_anom, obs_weight, coords = pack(prior_observation, slot_cells, gauge_count[:, :, batch], obs_value[:, :, batch], obs_noise[:, :, batch], obs_var[:, :, batch], tile_row, tile_col, TILE_ROWS_SIZE, TILE_COLUMNS)
        pad_spec = ((1, 1), (1, 1), (0, 0), (0, 0))
        anom_pad = jnp.pad(obs_anom, pad_spec)
        weight_pad = jnp.pad(obs_weight, pad_spec)
        coords_pad = jnp.pad(coords, pad_spec)
        present_state = predict_flood

        def one_tile(tile):
            row_at = (tile // N_COL).astype(jnp.int32)
            col_at = (tile % N_COL).astype(jnp.int32)
            start = (row_at, col_at, zero_index, zero_index)
            near_anom = lax.dynamic_slice(anom_pad, start, (3, 3, GT, ENSEMBLE_SIZE)).reshape(9 * GT, ENSEMBLE_SIZE)
            near_weight = lax.dynamic_slice(weight_pad, start, (3, 3, GT, ENSEMBLE_SIZE)).reshape(9 * GT, ENSEMBLE_SIZE)
            near_coords = lax.dynamic_slice(coords_pad, start, (3, 3, GT, 2)).reshape(9 * GT, 2)
            block = lax.dynamic_slice(present_state, (zero_index, zero_index, (row_at * TILE_ROWS_SIZE).astype(jnp.int32), (col_at * TILE_COLUMNS).astype(jnp.int32)), (3, ENSEMBLE_SIZE, TILE_ROWS_SIZE, TILE_COLUMNS)).reshape(3, ENSEMBLE_SIZE, TILE_ROWS_SIZE * TILE_COLUMNS)
            rows_here = (row_at * TILE_ROWS_SIZE + jnp.arange(TILE_ROWS_SIZE, dtype=jnp.int32)).astype(jnp.float32)
            cols_here = (col_at * TILE_COLUMNS + jnp.arange(TILE_COLUMNS, dtype=jnp.int32)).astype(jnp.float32)
            cell_rows = jnp.broadcast_to(rows_here[:, None], (TILE_ROWS_SIZE, TILE_COLUMNS)).reshape(-1)
            cell_cols = jnp.broadcast_to(cols_here[None, :], (TILE_ROWS_SIZE, TILE_COLUMNS)).reshape(-1)
            updated = block + increments(block, cell_rows, cell_cols, near_anom, near_weight, near_coords)
            return updated.reshape(3, ENSEMBLE_SIZE, TILE_ROWS_SIZE, TILE_COLUMNS)
        per_tile_state = lax.map(one_tile, jnp.arange(N_ROW * N_COL, dtype=jnp.int32))
        predict_flood = per_tile_state.reshape(N_ROW, N_COL, 3, ENSEMBLE_SIZE, TILE_ROWS_SIZE, TILE_COLUMNS).transpose(2, 3, 0, 4, 1, 5).reshape(3, ENSEMBLE_SIZE, GRID_ROWS, GRID_COLUMNS)
    return predict_flood
```

```python
import functools

import jax
import jax.numpy as jnp
from jax import lax
from jax.experimental import pallas as pl
from jax.experimental.pallas import tpu as pltpu
from jax.sharding import PartitionSpec as P

LOC = 6
GRAVITY = 9.81
SPACING = 2.0
STEP = 0.08
F32 = jnp.float32
BF16 = jnp.bfloat16
MESH = pl.DeviceIdType.MESH

TILES = [(dr, dc) for dc in (0, -1, 1) for dr in (-1, 0, 1)]
OWN = 1


def cell(h, n, t, vn, c):
    return (h, n, t, vn, vn - c, vn + c, (0.5 * GRAVITY) * h * h)


def face(lo, up):
    slow = jnp.minimum(jnp.minimum(lo[4], up[4]), 0.0)
    fast = jnp.maximum(jnp.maximum(lo[5], up[5]), 0.0)
    inv = 1.0 / (fast - slow)
    a = fast * inv
    b = slow * inv
    wl = a * (lo[3] - slow)
    wu = b * (fast - up[3])
    return (
        wl * lo[0] + wu * up[0],
        wl * lo[1] + wu * up[1] + (a * lo[6] - b * up[6]),
        wl * lo[2] + wu * up[2],
    )


def split2(x):
    hi = x.astype(BF16)
    return hi, (x - hi.astype(F32)).astype(BF16)


def kernel(
    x_ref, cells_ref, count_ref, value_ref, noise_ref, var_ref, out_ref,
    S, SEC, C, GR, OWNP, GC, META, PK, TC, TE, OH, OBS, RC, RE, INCE,
    row_send, row_recv, col_send, col_recv, meta_send, meta_recv, pk_send, pk_recv,
):
    n_row, n_col = lax.axis_size("row"), lax.axis_size("col")
    my_r, my_c = lax.axis_index("row"), lax.axis_index("col")
    rows, members, lanes = S.shape[1:]
    batches, slots = cells_ref.shape
    at_top, at_bottom = my_r == 0, my_r == n_row - 1
    at_left, at_right = my_c == 0, my_c == n_col - 1
    blocks = members // 8

    def present(dr, dc):
        ok = None
        for cond, d in ((my_r > 0, dr == -1), (my_r < n_row - 1, dr == 1),
                        (my_c > 0, dc == -1), (my_c < n_col - 1, dc == 1)):
            if d:
                ok = cond if ok is None else jnp.logical_and(ok, cond)
        return ok

    def device(dr, dc):
        return (jnp.clip(my_r + dr, 0, n_row - 1), jnp.clip(my_c + dc, 0, n_col - 1))

    others = [(k, dr, dc) for k, (dr, dc) in enumerate(TILES) if k != OWN]

    def mirror(k):
        dr, dc = TILES[k]
        return TILES.index((-dr, -dc))

    barrier = pltpu.get_barrier_semaphore()
    for k, dr, dc in others:
        @pl.when(present(dr, dc))
        def _(dr=dr, dc=dc):
            pl.semaphore_signal(barrier, inc=1, device_id=device(dr, dc), device_id_type=MESH)

    for r in (0, rows - 1) + tuple(range(1, rows - 1)):
        for f in range(3):
            S[f, r] = x_ref[f, pl.ds(r, members, stride=rows), :]

    near_r = 1 + (my_r > 0).astype(jnp.int32) + (my_r < n_row - 1).astype(jnp.int32)
    near_c = 1 + (my_c > 0).astype(jnp.int32) + (my_c < n_col - 1).astype(jnp.int32)
    pl.semaphore_wait(barrier, near_r * near_c - 1)

    def row_copies(stage, src):
        up = pltpu.make_async_remote_copy(
            src_ref=src.at[:, 0], dst_ref=GR.at[stage, 1],
            send_sem=row_send.at[stage, 0], recv_sem=row_recv.at[stage, 1],
            device_id=device(-1, 0), device_id_type=MESH)
        down = pltpu.make_async_remote_copy(
            src_ref=src.at[:, rows - 1], dst_ref=GR.at[stage, 0],
            send_sem=row_send.at[stage, 1], recv_sem=row_recv.at[stage, 0],
            device_id=device(1, 0), device_id_type=MESH)
        return up, down

    def row_start(stage, src):
        up, down = row_copies(stage, src)
        pl.when(my_r > 0)(up.start)
        pl.when(my_r < n_row - 1)(down.start)
        for side, r, wall in ((0, 0, at_top), (1, rows - 1, at_bottom)):
            @pl.when(wall)
            def _(side=side, r=r):
                GR[stage, side, 0] = src[0, r]
                GR[stage, side, 1] = src[1, r]
                GR[stage, side, 2] = -src[2, r]

    def row_wait(stage, src):
        up, down = row_copies(stage, src)

        @pl.when(my_r > 0)
        def _():
            up.wait_send()
            down_like = pltpu.make_async_remote_copy(
                src_ref=src.at[:, rows - 1], dst_ref=GR.at[stage, 0],
                send_sem=row_send.at[stage, 1], recv_sem=row_recv.at[stage, 0],
                device_id=device(-1, 0), device_id_type=MESH)
            down_like.wait_recv()

        @pl.when(my_r < n_row - 1)
        def _():
            down.wait_send()
            up_like = pltpu.make_async_remote_copy(
                src_ref=src.at[:, 0], dst_ref=GR.at[stage, 1],
                send_sem=row_send.at[stage, 0], recv_sem=row_recv.at[stage, 1],
                device_id=device(1, 0), device_id_type=MESH)
            up_like.wait_recv()

    def col_copies(stage):
        left = pltpu.make_async_remote_copy(
            src_ref=OWNP.at[stage], dst_ref=GC.at[stage, 1],
            send_sem=col_send.at[stage, 0], recv_sem=col_recv.at[stage, 1],
            device_id=device(0, -1), device_id_type=MESH)
        right = pltpu.make_async_remote_copy(
            src_ref=OWNP.at[stage], dst_ref=GC.at[stage, 0],
            send_sem=col_send.at[stage, 1], recv_sem=col_recv.at[stage, 0],
            device_id=device(0, 1), device_id_type=MESH)
        return left, right

    lane8 = lax.broadcasted_iota(jnp.int32, (8, lanes), 1)
    lane64 = lax.broadcasted_iota(jnp.int32, (members, lanes), 1)

    def col_start(stage, src):
        def pack(i, carry):
            m = pl.ds(pl.multiple_of(i * 8, 8), 8)
            packed = jnp.zeros((8, lanes), F32)
            for f in range(3):
                for r in range(rows):
                    k = f * rows + r
                    rolled = pltpu.roll(src[f, r, m, :], 2 * k + 1, 1)
                    packed = jnp.where(lane8 // 2 == k, rolled, packed)
            OWNP[stage, m, :] = packed
            return carry

        lax.fori_loop(0, blocks, pack, 0)
        left, right = col_copies(stage)
        pl.when(my_c > 0)(left.start)
        pl.when(my_c < n_col - 1)(right.start)
        flip = jnp.where((lane64 >= 2 * rows) & (lane64 < 4 * rows), -1.0, 1.0)

        @pl.when(at_left)
        def _():
            GC[stage, 0] = pltpu.roll(OWNP[stage], lanes - 1, 1) * flip

        @pl.when(at_right)
        def _():
            GC[stage, 1] = pltpu.roll(OWNP[stage], 1, 1) * flip

    def col_wait(stage):
        left, right = col_copies(stage)

        @pl.when(my_c > 0)
        def _():
            left.wait_send()
            right.wait_recv()

        @pl.when(my_c < n_col - 1)
        def _():
            right.wait_send()
            left.wait_recv()

    def advance(stage, src, first, last, finish):
        def body(i, carry):
            m = pl.ds(pl.multiple_of(i * 8, 8), 8)
            even = lane8 % 2 == 0
            own = OWNP[stage, m, :]
            lo = jnp.where(even, own, pltpu.roll(GC[stage, 0, m, :], 1, 1))
            up = jnp.where(even, pltpu.roll(GC[stage, 1, m, :], lanes - 1, 1), own)

            def unpack(v):
                h, n, t = v, pltpu.roll(v, lanes - 2 * rows, 1), pltpu.roll(v, lanes - 4 * rows, 1)
                return cell(h, n, t, n / h, jnp.sqrt(GRAVITY * h))

            edge = face(unpack(lo), unpack(up))

            def load(r):
                if r < 0:
                    f = [GR[stage, 0, f, m, :] for f in range(3)]
                elif r >= rows:
                    f = [GR[stage, 1, f, m, :] for f in range(3)]
                else:
                    f = [src[f, r, m, :] for f in range(3)]
                return f

            def derive(f):
                rec = 1.0 / f[0]
                return f[1] * rec, f[2] * rec, jnp.sqrt(GRAVITY * f[0])

            def rowcell(f, d):
                return cell(f[0], f[2], f[1], d[1], d[2])

            fb = load(first - 1)
            fc = load(first)
            dc = derive(fc)
            below = face(rowcell(fb, derive(fb)), rowcell(fc, dc))
            for r in range(first, last):
                fn = load(r + 1)
                dn = derive(fn)
                above = face(rowcell(fc, dc), rowcell(fn, dn))
                left = [pltpu.roll(v, 1, 1) for v in (*fc, dc[0], dc[2])]
                flux = face(cell(*left), cell(*fc, dc[0], dc[2]))
                out = []
                for f, g in ((0, 0), (1, 2), (2, 1)):
                    q = pltpu.roll(edge[f], lanes - 1 - 2 * r, 1)
                    low = jnp.where(lane8 == 0, q, flux[f])
                    high = jnp.where(lane8 == lanes - 1, q, pltpu.roll(low, lanes - 1, 1))
                    out.append((high - low + above[g] - below[g]) * (-1.0 / SPACING))
                finish(r, m, fc, out)
                fc, dc, below = fn, dn, above
            return carry

        lax.fori_loop(0, blocks, body, 0)

    def finish1(r, m, fields, tend):
        for f in range(3):
            SEC[f, r, m, :] = fields[f] + STEP * tend[f]

    def finish2(r, m, fields, tend):
        for f in range(3):
            C[f, r, m, :] = 0.5 * (S[f, r, m, :] + fields[f] + STEP * tend[f])

    row_start(0, S)
    META[OWN] = jnp.zeros((8, lanes), F32)
    META[OWN, 0:batches, 0:slots] = cells_ref[...].astype(F32)
    col_start(0, S)

    def meta_copy(k, dr, dc):
        return pltpu.make_async_remote_copy(
            src_ref=META.at[OWN], dst_ref=META.at[mirror(k)],
            send_sem=meta_send.at[k], recv_sem=meta_recv.at[mirror(k)],
            device_id=device(dr, dc), device_id_type=MESH)

    def pk_copy(b, k, dr, dc):
        return pltpu.make_async_remote_copy(
            src_ref=PK.at[b, OWN], dst_ref=PK.at[b, mirror(k)],
            send_sem=pk_send.at[b, k], recv_sem=pk_recv.at[b, mirror(k)],
            device_id=device(dr, dc), device_id_type=MESH)

    for k, dr, dc in others:
        @pl.when(present(dr, dc))
        def _(k=k, dr=dr, dc=dc):
            meta_copy(k, dr, dc).start()

        @pl.when(jnp.logical_not(present(dr, dc)))
        def _(k=k):
            META[k] = jnp.zeros((8, lanes), F32)
            for b in range(batches):
                PK[b, k] = jnp.zeros((slots, lanes), F32)

    eye = lax.broadcasted_iota(jnp.int32, (slots, lanes), 0) == lax.broadcasted_iota(
        jnp.int32, (slots, lanes), 1)

    def column(row):
        return jnp.sum(jnp.where(eye, row, 0.0), axis=1, keepdims=True)

    lane_s = lax.broadcasted_iota(jnp.int32, (slots, lanes), 1).astype(F32)
    wide = lambda row: jnp.concatenate([row, jnp.zeros((1, lanes - slots), F32)], axis=1)
    for b in range(batches):
        own_cell = column(META[OWN, b:b + 1, :])
        for r in range(rows):
            OH[b, :, r * lanes:(r + 1) * lanes] = jnp.where(
                own_cell == lane_s + float(r * lanes), 1.0, 0.0).astype(BF16)
        OBS[b, 0] = jnp.broadcast_to(column(wide(value_ref[b:b + 1, :])), (slots, lanes))
        OBS[b, 1] = jnp.broadcast_to(column(wide(var_ref[b:b + 1, :])), (slots, lanes))

    col_wait(0)
    advance(0, S, 1, rows - 1, finish1)
    row_wait(0, S)
    advance(0, S, 0, 1, finish1)
    advance(0, S, rows - 1, rows, finish1)

    row_start(1, SEC)
    col_start(1, SEC)

    for k, dr, dc in others:
        @pl.when(present(dr, dc))
        def _(k=k, dr=dr, dc=dc):
            meta_copy(k, dr, dc).wait_send()
            meta_copy(mirror(k), -dr, -dc).wait_recv()

    window = 2 * LOC
    members_1 = float(members - 1)
    lane_1 = lax.broadcasted_iota(jnp.int32, (1, lanes), 1)
    in_window = lane_1 % window
    edge_row = (lane_1 // window).astype(F32)
    edge_col = jnp.where(in_window < LOC, lanes - LOC + in_window, in_window - LOC).astype(F32)
    inv_loc = 1.0 / (LOC * LOC)
    for b in range(batches):
        for k, (dr, dc) in enumerate(TILES):
            at = column(META[k, b:b + 1, :])
            g_row = jnp.floor(at * (1.0 / lanes))
            g_col = at - g_row * lanes + float(dc * lanes)
            g_row = g_row + float(dr * rows)
            where = pl.ds((k % 3) * slots, slots)
            if dc == 0:
                dcol = lane_s - g_col
                dcol = dcol * dcol
                for r in range(rows):
                    drow = float(r) - g_row
                    t = jnp.maximum(1.0 - (dcol + drow * drow) * inv_loc, 0.0)
                    TC[b, where, r * lanes:(r + 1) * lanes] = t * t * (1.0 / members_1)
            else:
                dcol = edge_col - g_col
                drow = edge_row - g_row
                t = jnp.maximum(1.0 - (dcol * dcol + drow * drow) * inv_loc, 0.0)
                TE[b, (k - 3) * slots:(k - 2) * slots, :] = t * t * (1.0 / members_1)

    col_wait(1)
    advance(1, SEC, 1, rows - 1, finish2)
    row_wait(1, SEC)
    advance(1, SEC, 0, 1, finish2)
    advance(1, SEC, rows - 1, rows, finish2)

    dot = functools.partial(lax.dot_general, preferred_element_type=F32)
    nn = (((1,), (0,)), ((), ()))
    nt = (((1,), (1,)), ((), ()))

    def operands(packets):
        lane = lax.broadcasted_iota(jnp.int32, packets.shape, 1)
        swapped = pltpu.roll(packets, lanes // 2, 1)
        anom = jnp.where(lane < members, packets, swapped)
        weight = jnp.where(lane < members, swapped, packets)
        hi, lo = split2(anom)
        w_hi = weight.astype(BF16).astype(F32)
        w = jnp.where(lane < members, w_hi, weight - w_hi)
        return (jnp.concatenate([hi, lo], axis=1),
                jnp.concatenate([w, w], axis=0).T.astype(BF16))

    def increment(anom, weight, centred, taper):
        cov = dot(anom, centred, nn) * taper
        hi, lo = split2(cov)
        both = dot(weight, jnp.concatenate([hi, lo], axis=0), nn)
        return both[:members] + both[members:]

    def centre(v):
        hi, lo = split2(v - jnp.mean(v, axis=0, keepdims=True))
        return jnp.concatenate([hi, lo, hi, lo], axis=0)

    for b in range(batches):
        depth = jnp.concatenate([C[0, r] for r in range(rows)], axis=1)
        hi, rest = depth.astype(BF16), None
        rest = depth - hi.astype(F32)
        mid, low = split2(rest)
        onehot = OH[b]
        prior = dot(onehot, hi, nt) + (dot(onehot, mid, nt) + dot(onehot, low, nt))
        anom = prior - jnp.mean(prior, axis=1, keepdims=True)
        spread = jnp.sum(anom * anom, axis=1, keepdims=True) * (1.0 / members_1)
        slot = lax.broadcasted_iota(jnp.int32, (slots, members), 0)
        live = jnp.where(slot < count_ref[0, 0, b], 1.0, 0.0)
        weight = live * (OBS[b, 0, :, :members] + noise_ref[b] - prior) / (
            spread + OBS[b, 1, :, :members])
        PK[b, OWN] = jnp.concatenate([anom, weight], axis=1)
        for k, dr, dc in others:
            @pl.when(present(dr, dc))
            def _(k=k, dr=dr, dc=dc):
                pk_copy(b, k, dr, dc).start()

        def prepare(f, carry):
            edges = jnp.zeros((members, lanes), F32)
            for r in range(rows):
                rolled = pltpu.roll(C[f, r], window * r + LOC, 1)
                edges = jnp.where(lane64 // window == r, rolled, edges)
            RE[f] = centre(edges)
            for pair in range(rows // 2):
                v = jnp.concatenate([C[f, 2 * pair], C[f, 2 * pair + 1]], axis=1)
                RC[f, pair] = centre(v)
            return carry

        lax.fori_loop(0, 3, prepare, 0)

        def arrive(ks):
            for k, dr, dc in others:
                if k in ks:
                    @pl.when(present(dr, dc))
                    def _(k=k, dr=dr, dc=dc):
                        pk_copy(b, k, dr, dc).wait_send()
                        pk_copy(b, mirror(k), -dr, -dc).wait_recv()

        arrive((0, 2))
        anom_c, weight_c = operands(PK[b, 0:3].reshape(3 * slots, lanes))

        def update(f, carry):
            for pair in range(rows // 2):
                span = slice(2 * pair * lanes, (2 * pair + 2) * lanes)
                inc = increment(anom_c, weight_c, RC[f, pair], TC[b, :, span])
                C[f, 2 * pair] = C[f, 2 * pair] + inc[:, :lanes]
                C[f, 2 * pair + 1] = C[f, 2 * pair + 1] + inc[:, lanes:]
            return carry

        lax.fori_loop(0, 3, update, 0)
        arrive((3, 4, 5, 6, 7, 8))
        anom_e, weight_e = operands(PK[b, 3:9].reshape(6 * slots, lanes))

        def update_edges(f, carry):
            inc = increment(anom_e, weight_e, RE[f], TE[b])
            outer = (lane64 < LOC) | (lane64 >= lanes - LOC)
            for r in range(rows):
                back = pltpu.roll(inc, (lanes - (window * r + LOC)) % lanes, 1)
                done = C[f, r] + jnp.where(outer, back, 0.0)
                if b < batches - 1:
                    C[f, r] = done
                else:
                    out_ref[f, pl.ds(r, members, stride=rows), :] = done
            return carry

        lax.fori_loop(0, 3, update_edges, 0)


def body(state, gauge_cells, gauge_count, obs_value, obs_noise, obs_var):
    fields, members, rows, lanes = state.shape
    batches, slots = gauge_cells.shape[2:]
    vmem = pl.BlockSpec(memory_space=pltpu.VMEM)
    dma = pltpu.SemaphoreType.DMA
    grid = (fields, rows, members, lanes)
    out = pl.pallas_call(
        kernel,
        out_shape=jax.ShapeDtypeStruct((fields, members * rows, lanes), F32),
        in_specs=[vmem, vmem, pl.BlockSpec(memory_space=pltpu.SMEM), vmem, vmem, vmem],
        out_specs=vmem,
        scratch_shapes=[
            pltpu.VMEM(grid, F32),
            pltpu.VMEM(grid, F32),
            pltpu.VMEM(grid, F32),
            pltpu.VMEM((2, 2, fields, members, lanes), F32),
            pltpu.VMEM((2, members, lanes), F32),
            pltpu.VMEM((2, 2, members, lanes), F32),
            pltpu.VMEM((9, 8, lanes), F32),
            pltpu.VMEM((batches, 9, slots, lanes), F32),
            pltpu.VMEM((batches, 3 * slots, rows * lanes), F32),
            pltpu.VMEM((batches, 6 * slots, lanes), F32),
            pltpu.VMEM((batches, slots, rows * lanes), BF16),
            pltpu.VMEM((batches, 2, slots, lanes), F32),
            pltpu.VMEM((fields, rows // 2, 4 * members, 2 * lanes), BF16),
            pltpu.VMEM((fields, 4 * members, lanes), BF16),
            pltpu.VMEM((fields, members, lanes), F32),
            dma((2, 2)), dma((2, 2)), dma((2, 2)), dma((2, 2)),
            dma((9,)), dma((9,)), dma((batches, 9)), dma((batches, 9)),
        ],
        compiler_params=pltpu.CompilerParams(
            collective_id=0, has_side_effects=True, vmem_limit_bytes=40 * 1024 * 1024),
    )(
        state.reshape(fields, members * rows, lanes),
        gauge_cells.reshape(batches, slots),
        gauge_count,
        obs_value.reshape(batches, slots),
        obs_noise.reshape(batches, slots, members),
        obs_var.reshape(batches, slots),
    )
    return out.reshape(state.shape)


def solution(mesh):
    placed = (
        P(None, None, "row", "col"),
        P("row", "col", None, None),
        P("row", "col", None),
        P("row", "col", None, None),
        P("row", "col", None, None, None),
        P("row", "col", None, None),
    )
    return jax.shard_map(
        body, mesh=mesh, in_specs=placed, out_specs=P(None, None, "row", "col"), check_vma=False
    )
```

```python
import functools

import jax
import jax.numpy as jnp
from jax import lax
from jax.experimental import pallas as pl
from jax.experimental.pallas import tpu as pltpu
from jax.sharding import PartitionSpec as P

LOC = 6
GRAVITY = 9.81
SPACING = 2.0
STEP = 0.08
ROOT_G = GRAVITY ** 0.5
INNER = 16
OUTER = 32
F32 = jnp.float32
BF16 = jnp.bfloat16
MESH = pl.DeviceIdType.MESH

TILES = [(dr, dc) for dc in (0, -1, 1) for dr in (-1, 0, 1)]
OWN = 1


def cell(h, n, t, vn, c):
    return (h, n, t, vn, vn - c, vn + c, (0.5 * GRAVITY) * h * h)


def face(lo, up):
    slow = jnp.minimum(jnp.minimum(lo[4], up[4]), 0.0)
    fast = jnp.maximum(jnp.maximum(lo[5], up[5]), 0.0)
    inv = 1.0 / (fast - slow)
    a = fast * inv
    b = slow * inv
    wl = a * (lo[3] - slow)
    wu = b * (fast - up[3])
    return (
        wl * lo[0] + wu * up[0],
        wl * lo[1] + wu * up[1] + (a * lo[6] - b * up[6]),
        wl * lo[2] + wu * up[2],
    )


def split2(x):
    hi = x.astype(BF16)
    return hi, (x - hi.astype(F32)).astype(BF16)


def kernel(
    x_hbm, cells_hbm, count_ref, value_hbm, noise_hbm, var_hbm, out_ref,
    x_ref, cells_ref, value_ref, noise_ref, var_ref,
    S, SEC, C, GR, OWNP, GC, META, PK, TC, TE, OH, OBS, RC, RE, EF,
    in_sem, row_send, row_recv, col_send, col_recv, meta_send, meta_recv, pk_send, pk_recv,
):
    n_row, n_col = lax.axis_size("row"), lax.axis_size("col")
    my_r, my_c = lax.axis_index("row"), lax.axis_index("col")
    rows, members, lanes = S.shape[1:]
    batches, slots = cells_ref.shape
    at_top, at_bottom = my_r == 0, my_r == n_row - 1
    at_left, at_right = my_c == 0, my_c == n_col - 1
    blocks = members // 8

    def present(dr, dc):
        ok = None
        for cond, d in ((my_r > 0, dr == -1), (my_r < n_row - 1, dr == 1),
                        (my_c > 0, dc == -1), (my_c < n_col - 1, dc == 1)):
            if d:
                ok = cond if ok is None else jnp.logical_and(ok, cond)
        return ok

    def device(dr, dc):
        return (jnp.clip(my_r + dr, 0, n_row - 1), jnp.clip(my_c + dc, 0, n_col - 1))

    others = [(k, dr, dc) for k, (dr, dc) in enumerate(TILES) if k != OWN]

    def mirror(k):
        dr, dc = TILES[k]
        return TILES.index((-dr, -dc))

    loads = [
        pltpu.make_async_copy(a, b, in_sem.at[i]) for i, (a, b) in enumerate((
            (x_hbm, x_ref), (cells_hbm, cells_ref), (value_hbm, value_ref),
            (noise_hbm, noise_ref), (var_hbm, var_ref)))]
    for load in loads:
        load.start()

    barrier = pltpu.get_barrier_semaphore()
    for k, dr, dc in others:
        @pl.when(present(dr, dc))
        def _(dr=dr, dc=dc):
            pl.semaphore_signal(barrier, inc=1, device_id=device(dr, dc), device_id_type=MESH)

    loads[0].wait()
    for r in (0, rows - 1) + tuple(range(1, rows - 1)):
        for f in range(3):
            S[f, r] = x_ref[f, pl.ds(r, members, stride=rows), :]

    near_r = 1 + (my_r > 0).astype(jnp.int32) + (my_r < n_row - 1).astype(jnp.int32)
    near_c = 1 + (my_c > 0).astype(jnp.int32) + (my_c < n_col - 1).astype(jnp.int32)
    pl.semaphore_wait(barrier, near_r * near_c - 1)

    def row_copies(stage, src):
        up = pltpu.make_async_remote_copy(
            src_ref=src.at[:, 0], dst_ref=GR.at[stage, 1],
            send_sem=row_send.at[stage, 0], recv_sem=row_recv.at[stage, 1],
            device_id=device(-1, 0), device_id_type=MESH)
        down = pltpu.make_async_remote_copy(
            src_ref=src.at[:, rows - 1], dst_ref=GR.at[stage, 0],
            send_sem=row_send.at[stage, 1], recv_sem=row_recv.at[stage, 0],
            device_id=device(1, 0), device_id_type=MESH)
        return up, down

    def row_start(stage, src):
        up, down = row_copies(stage, src)
        pl.when(my_r > 0)(up.start)
        pl.when(my_r < n_row - 1)(down.start)
        for side, r, wall in ((0, 0, at_top), (1, rows - 1, at_bottom)):
            @pl.when(wall)
            def _(side=side, r=r):
                GR[stage, side, 0] = src[0, r]
                GR[stage, side, 1] = src[1, r]
                GR[stage, side, 2] = -src[2, r]

    def row_wait(stage, src):
        up, down = row_copies(stage, src)

        @pl.when(my_r > 0)
        def _():
            up.wait_send()
            down_like = pltpu.make_async_remote_copy(
                src_ref=src.at[:, rows - 1], dst_ref=GR.at[stage, 0],
                send_sem=row_send.at[stage, 1], recv_sem=row_recv.at[stage, 0],
                device_id=device(-1, 0), device_id_type=MESH)
            down_like.wait_recv()

        @pl.when(my_r < n_row - 1)
        def _():
            down.wait_send()
            up_like = pltpu.make_async_remote_copy(
                src_ref=src.at[:, 0], dst_ref=GR.at[stage, 1],
                send_sem=row_send.at[stage, 0], recv_sem=row_recv.at[stage, 1],
                device_id=device(1, 0), device_id_type=MESH)
            up_like.wait_recv()

    def col_copies(stage):
        left = pltpu.make_async_remote_copy(
            src_ref=OWNP.at[stage], dst_ref=GC.at[stage, 1],
            send_sem=col_send.at[stage, 0], recv_sem=col_recv.at[stage, 1],
            device_id=device(0, -1), device_id_type=MESH)
        right = pltpu.make_async_remote_copy(
            src_ref=OWNP.at[stage], dst_ref=GC.at[stage, 0],
            send_sem=col_send.at[stage, 1], recv_sem=col_recv.at[stage, 0],
            device_id=device(0, 1), device_id_type=MESH)
        return left, right

    lane8 = lax.broadcasted_iota(jnp.int32, (8, lanes), 1)
    lane32 = lax.broadcasted_iota(jnp.int32, (32, lanes), 1)
    lane64 = lax.broadcasted_iota(jnp.int32, (members, lanes), 1)

    def col_start(stage, src):
        def pack(i, carry):
            m = pl.ds(pl.multiple_of(i * 32, 8), 32)
            packed = jnp.zeros((32, lanes), F32)
            for f in range(3):
                for r in range(rows):
                    k = f * rows + r
                    rolled = pltpu.roll(src[f, r, m, :], 2 * k + 1, 1)
                    packed = jnp.where(lane32 // 2 == k, rolled, packed)
            OWNP[stage, m, :] = packed
            return carry

        lax.fori_loop(0, members // 32, pack, 0)
        left, right = col_copies(stage)
        pl.when(my_c > 0)(left.start)
        pl.when(my_c < n_col - 1)(right.start)
        flip = jnp.where((lane64 >= 2 * rows) & (lane64 < 4 * rows), -1.0, 1.0)

        @pl.when(at_left)
        def _():
            GC[stage, 0] = pltpu.roll(OWNP[stage], lanes - 1, 1) * flip

        @pl.when(at_right)
        def _():
            GC[stage, 1] = pltpu.roll(OWNP[stage], 1, 1) * flip

    def col_wait(stage):
        left, right = col_copies(stage)

        @pl.when(my_c > 0)
        def _():
            left.wait_send()
            right.wait_recv()

        @pl.when(my_c < n_col - 1)
        def _():
            right.wait_send()
            left.wait_recv()

    def edge_flux(stage):
        even = lax.broadcasted_iota(jnp.int32, (32, lanes), 1) % 2 == 0

        def body(i, carry):
            m = pl.ds(pl.multiple_of(i * 32, 8), 32)
            own = OWNP[stage, m, :]
            lo = jnp.where(even, own, pltpu.roll(GC[stage, 0, m, :], 1, 1))
            up = jnp.where(even, pltpu.roll(GC[stage, 1, m, :], lanes - 1, 1), own)

            def unpack(v):
                h, n, t = v, pltpu.roll(v, lanes - 2 * rows, 1), pltpu.roll(v, lanes - 4 * rows, 1)
                rs = lax.rsqrt(h)
                return cell(h, n, t, n * (rs * rs), ROOT_G * (h * rs))

            done = face(unpack(lo), unpack(up))
            for f in range(3):
                EF[f, m, :] = done[f]
            return carry

        lax.fori_loop(0, members // 32, body, 0)

    def advance(stage, src, tall, spans, finish):
        lane_b = lax.broadcasted_iota(jnp.int32, (tall, lanes), 1)

        def body(i, carry):
            m = pl.ds(pl.multiple_of(i * tall, 8), tall)
            edge = [EF[f, m, :] for f in range(3)]

            def load(r):
                if r < 0:
                    f = [GR[stage, 0, f, m, :] for f in range(3)]
                elif r >= rows:
                    f = [GR[stage, 1, f, m, :] for f in range(3)]
                else:
                    f = [src[f, r, m, :] for f in range(3)]
                return f

            def derive(f):
                rs = lax.rsqrt(f[0])
                rec = rs * rs
                return f[1] * rec, f[2] * rec, ROOT_G * (f[0] * rs)

            def rowcell(f, d):
                return cell(f[0], f[2], f[1], d[1], d[2])

            for first, last in spans:
                fb = load(first - 1)
                fc = load(first)
                dc = derive(fc)
                below = face(rowcell(fb, derive(fb)), rowcell(fc, dc))
                for r in range(first, last):
                    fn = load(r + 1)
                    dn = derive(fn)
                    above = face(rowcell(fc, dc), rowcell(fn, dn))
                    left = [pltpu.roll(v, 1, 1) for v in (*fc, dc[0], dc[2])]
                    flux = face(cell(*left), cell(*fc, dc[0], dc[2]))
                    out = []
                    for f, g in ((0, 0), (1, 2), (2, 1)):
                        q = pltpu.roll(edge[f], lanes - 1 - 2 * r, 1)
                        low = jnp.where(lane_b == 0, q, flux[f])
                        high = jnp.where(lane_b == lanes - 1, q, pltpu.roll(low, lanes - 1, 1))
                        out.append((high - low + above[g] - below[g]) * (-1.0 / SPACING))
                    finish(r, m, fc, out)
                    fc, dc, below = fn, dn, above
            return carry

        lax.fori_loop(0, members // tall, body, 0)

    def finish1(r, m, fields, tend):
        for f in range(3):
            SEC[f, r, m, :] = fields[f] + STEP * tend[f]

    def finish2(r, m, fields, tend):
        for f in range(3):
            C[f, r, m, :] = 0.5 * (S[f, r, m, :] + fields[f] + STEP * tend[f])

    row_start(0, S)
    for load in loads[1:]:
        load.wait()
    META[OWN] = jnp.zeros((8, lanes), F32)
    META[OWN, 0:batches, 0:slots] = cells_ref[...].astype(F32)
    col_start(0, S)

    def meta_copy(k, dr, dc):
        return pltpu.make_async_remote_copy(
            src_ref=META.at[OWN], dst_ref=META.at[mirror(k)],
            send_sem=meta_send.at[k], recv_sem=meta_recv.at[mirror(k)],
            device_id=device(dr, dc), device_id_type=MESH)

    def pk_copy(b, k, dr, dc):
        return pltpu.make_async_remote_copy(
            src_ref=PK.at[b, OWN], dst_ref=PK.at[b, mirror(k)],
            send_sem=pk_send.at[b, k], recv_sem=pk_recv.at[b, mirror(k)],
            device_id=device(dr, dc), device_id_type=MESH)

    for k, dr, dc in others:
        @pl.when(present(dr, dc))
        def _(k=k, dr=dr, dc=dc):
            meta_copy(k, dr, dc).start()

        @pl.when(jnp.logical_not(present(dr, dc)))
        def _(k=k):
            META[k] = jnp.zeros((8, lanes), F32)
            for b in range(batches):
                PK[b, k] = jnp.zeros((slots, lanes), F32)

    eye = lax.broadcasted_iota(jnp.int32, (slots, lanes), 0) == lax.broadcasted_iota(
        jnp.int32, (slots, lanes), 1)

    def column(row):
        return jnp.sum(jnp.where(eye, row, 0.0), axis=1, keepdims=True)

    lane_s = lax.broadcasted_iota(jnp.int32, (slots, lanes), 1).astype(F32)
    wide = lambda row: jnp.concatenate([row, jnp.zeros((1, lanes - slots), F32)], axis=1)
    for b in range(batches):
        own_cell = column(META[OWN, b:b + 1, :])
        for r in range(rows):
            OH[b, :, r * lanes:(r + 1) * lanes] = jnp.where(
                own_cell == lane_s + float(r * lanes), 1.0, 0.0).astype(BF16)
        OBS[b, 0] = jnp.broadcast_to(column(wide(value_ref[b:b + 1, :])), (slots, lanes))
        OBS[b, 1] = jnp.broadcast_to(column(wide(var_ref[b:b + 1, :])), (slots, lanes))

    col_wait(0)
    edge_flux(0)
    advance(0, S, INNER, ((1, rows - 1),), finish1)
    row_wait(0, S)
    advance(0, S, OUTER, ((0, 1), (rows - 1, rows)), finish1)

    row_start(1, SEC)
    col_start(1, SEC)

    for k, dr, dc in others:
        @pl.when(present(dr, dc))
        def _(k=k, dr=dr, dc=dc):
            meta_copy(k, dr, dc).wait_send()
            meta_copy(mirror(k), -dr, -dc).wait_recv()

    window = 2 * LOC
    members_1 = float(members - 1)
    lane_1 = lax.broadcasted_iota(jnp.int32, (1, lanes), 1)
    in_window = lane_1 % window
    edge_row = (lane_1 // window).astype(F32)
    edge_col = jnp.where(in_window < LOC, lanes - LOC + in_window, in_window - LOC).astype(F32)
    inv_loc = 1.0 / (LOC * LOC)
    for b in range(batches):
        for k, (dr, dc) in enumerate(TILES):
            at = column(META[k, b:b + 1, :])
            g_row = jnp.floor(at * (1.0 / lanes))
            g_col = at - g_row * lanes + float(dc * lanes)
            g_row = g_row + float(dr * rows)
            where = pl.ds((k % 3) * slots, slots)
            if dc == 0:
                dcol = lane_s - g_col
                dcol = dcol * dcol
                for r in range(rows):
                    drow = float(r) - g_row
                    t = jnp.maximum(1.0 - (dcol + drow * drow) * inv_loc, 0.0)
                    TC[b, where, r * lanes:(r + 1) * lanes] = t * t * (1.0 / members_1)
            else:
                dcol = edge_col - g_col
                drow = edge_row - g_row
                t = jnp.maximum(1.0 - (dcol * dcol + drow * drow) * inv_loc, 0.0)
                TE[b, (k - 3) * slots:(k - 2) * slots, :] = t * t * (1.0 / members_1)

    col_wait(1)
    edge_flux(1)
    advance(1, SEC, INNER, ((1, rows - 1),), finish2)
    row_wait(1, SEC)
    advance(1, SEC, OUTER, ((0, 1), (rows - 1, rows)), finish2)

    dot = functools.partial(lax.dot_general, preferred_element_type=F32)
    nn = (((1,), (0,)), ((), ()))
    nt = (((1,), (1,)), ((), ()))

    def operands(packets):
        lane = lax.broadcasted_iota(jnp.int32, packets.shape, 1)
        swapped = pltpu.roll(packets, lanes // 2, 1)
        anom = jnp.where(lane < members, packets, swapped)
        weight = jnp.where(lane < members, swapped, packets)
        hi, lo = split2(anom)
        w_hi = weight.astype(BF16).astype(F32)
        w = jnp.where(lane < members, w_hi, weight - w_hi)
        return (jnp.concatenate([hi, lo], axis=1),
                jnp.concatenate([w, w], axis=0).T.astype(BF16))

    def increment(anom, weight, centred, taper):
        cov = dot(anom, centred, nn) * taper
        hi, lo = split2(cov)
        both = dot(weight, jnp.concatenate([hi, lo], axis=0), nn)
        return both[:members] + both[members:]

    def centre(v):
        hi, lo = split2(v - jnp.mean(v, axis=0, keepdims=True))
        return jnp.concatenate([hi, lo, hi, lo], axis=0)

    for b in range(batches):
        depth = jnp.concatenate([C[0, r] for r in range(rows)], axis=1)
        hi, rest = depth.astype(BF16), None
        rest = depth - hi.astype(F32)
        mid, low = split2(rest)
        onehot = OH[b]
        prior = dot(onehot, hi, nt) + (dot(onehot, mid, nt) + dot(onehot, low, nt))
        anom = prior - jnp.mean(prior, axis=1, keepdims=True)
        spread = jnp.sum(anom * anom, axis=1, keepdims=True) * (1.0 / members_1)
        slot = lax.broadcasted_iota(jnp.int32, (slots, members), 0)
        live = jnp.where(slot < count_ref[0, 0, b], 1.0, 0.0)
        weight = live * (OBS[b, 0, :, :members] + noise_ref[b] - prior) / (
            spread + OBS[b, 1, :, :members])
        PK[b, OWN] = jnp.concatenate([anom, weight], axis=1)
        for k, dr, dc in others:
            @pl.when(present(dr, dc))
            def _(k=k, dr=dr, dc=dc):
                pk_copy(b, k, dr, dc).start()

        def prepare(f, carry):
            edges = jnp.zeros((members, lanes), F32)
            for r in range(rows):
                rolled = pltpu.roll(C[f, r], window * r + LOC, 1)
                edges = jnp.where(lane64 // window == r, rolled, edges)
            RE[f] = centre(edges)
            for pair in range(rows // 2):
                v = jnp.concatenate([C[f, 2 * pair], C[f, 2 * pair + 1]], axis=1)
                RC[f, pair] = centre(v)
            return carry

        for f in range(3):
            prepare(f, 0)

        def arrive(ks):
            for k, dr, dc in others:
                if k in ks:
                    @pl.when(present(dr, dc))
                    def _(k=k, dr=dr, dc=dc):
                        pk_copy(b, k, dr, dc).wait_send()
                        pk_copy(b, mirror(k), -dr, -dc).wait_recv()

        arrive((0, 2))
        anom_c, weight_c = operands(PK[b, 0:3].reshape(3 * slots, lanes))

        def update(f, carry):
            for pair in range(rows // 2):
                span = slice(2 * pair * lanes, (2 * pair + 2) * lanes)
                inc = increment(anom_c, weight_c, RC[f, pair], TC[b, :, span])
                C[f, 2 * pair] = C[f, 2 * pair] + inc[:, :lanes]
                C[f, 2 * pair + 1] = C[f, 2 * pair + 1] + inc[:, lanes:]
            return carry

        for f in range(3):
            update(f, 0)
        arrive((3, 4, 5, 6, 7, 8))
        anom_e, weight_e = operands(PK[b, 3:9].reshape(6 * slots, lanes))

        def update_edges(f, carry):
            inc = increment(anom_e, weight_e, RE[f], TE[b])
            outer = (lane64 < LOC) | (lane64 >= lanes - LOC)
            for r in range(rows):
                back = pltpu.roll(inc, (lanes - (window * r + LOC)) % lanes, 1)
                done = C[f, r] + jnp.where(outer, back, 0.0)
                if b < batches - 1:
                    C[f, r] = done
                else:
                    out_ref[f, pl.ds(r, members, stride=rows), :] = done
            return carry

        for f in range(3):
            update_edges(f, 0)


def body(state, gauge_cells, gauge_count, obs_value, obs_noise, obs_var):
    fields, members, rows, lanes = state.shape
    batches, slots = gauge_cells.shape[2:]
    vmem = pl.BlockSpec(memory_space=pltpu.VMEM)
    hbm = pl.BlockSpec(memory_space=pltpu.HBM)
    dma = pltpu.SemaphoreType.DMA
    grid = (fields, rows, members, lanes)
    out = pl.pallas_call(
        kernel,
        out_shape=jax.ShapeDtypeStruct((fields, members * rows, lanes), F32),
        in_specs=[hbm, hbm, pl.BlockSpec(memory_space=pltpu.SMEM), hbm, hbm, hbm],
        out_specs=vmem,
        scratch_shapes=[
            pltpu.VMEM((fields, members * rows, lanes), F32),
            pltpu.VMEM((batches, slots), gauge_cells.dtype),
            pltpu.VMEM((batches, slots), F32),
            pltpu.VMEM((batches, slots, members), F32),
            pltpu.VMEM((batches, slots), F32),
            pltpu.VMEM(grid, F32),
            pltpu.VMEM(grid, F32),
            pltpu.VMEM(grid, F32),
            pltpu.VMEM((2, 2, fields, members, lanes), F32),
            pltpu.VMEM((2, members, lanes), F32),
            pltpu.VMEM((2, 2, members, lanes), F32),
            pltpu.VMEM((9, 8, lanes), F32),
            pltpu.VMEM((batches, 9, slots, lanes), F32),
            pltpu.VMEM((batches, 3 * slots, rows * lanes), F32),
            pltpu.VMEM((batches, 6 * slots, lanes), F32),
            pltpu.VMEM((batches, slots, rows * lanes), BF16),
            pltpu.VMEM((batches, 2, slots, lanes), F32),
            pltpu.VMEM((fields, rows // 2, 4 * members, 2 * lanes), BF16),
            pltpu.VMEM((fields, 4 * members, lanes), BF16),
            pltpu.VMEM((fields, members, lanes), F32),
            dma((5,)),
            dma((2, 2)), dma((2, 2)), dma((2, 2)), dma((2, 2)),
            dma((9,)), dma((9,)), dma((batches, 9)), dma((batches, 9)),
        ],
        compiler_params=pltpu.CompilerParams(
            collective_id=0, has_side_effects=True, vmem_limit_bytes=40 * 1024 * 1024),
    )(
        state.reshape(fields, members * rows, lanes),
        gauge_cells.reshape(batches, slots),
        gauge_count,
        obs_value.reshape(batches, slots),
        obs_noise.reshape(batches, slots, members),
        obs_var.reshape(batches, slots),
    )
    return out.reshape(state.shape)


def solution(mesh):
    placed = (
        P(None, None, "row", "col"),
        P("row", "col", None, None),
        P("row", "col", None),
        P("row", "col", None, None),
        P("row", "col", None, None, None),
        P("row", "col", None, None),
    )
    return jax.shard_map(
        body, mesh=mesh, in_specs=placed, out_specs=P(None, None, "row", "col"), check_vma=False
    )
```

```python
import functools

import jax
import jax.numpy as jnp
from jax import lax
from jax.experimental import pallas as pl
from jax.experimental.pallas import tpu as pltpu
from jax.sharding import PartitionSpec as P

LOC = 6
GRAVITY = 9.81
SPACING = 2.0
STEP = 0.08
ROOT_G = GRAVITY ** 0.5
INNER = 16
OUTER = 64
F32 = jnp.float32
BF16 = jnp.bfloat16
MESH = pl.DeviceIdType.MESH

TILES = [(dr, dc) for dc in (0, -1, 1) for dr in (-1, 0, 1)]
OWN = 1


def cell(h, n, t, vn, c):
    return (h, n, t, vn, vn - c, vn + c, (0.5 * GRAVITY) * h * h)


def face(lo, up):
    slow = jnp.minimum(jnp.minimum(lo[4], up[4]), 0.0)
    fast = jnp.maximum(jnp.maximum(lo[5], up[5]), 0.0)
    inv = 1.0 / (fast - slow)
    a = fast * inv
    b = slow * inv
    wl = a * (lo[3] - slow)
    wu = b * (fast - up[3])
    return (
        wl * lo[0] + wu * up[0],
        wl * lo[1] + wu * up[1] + (a * lo[6] - b * up[6]),
        wl * lo[2] + wu * up[2],
    )


def split2(x):
    hi = x.astype(BF16)
    return hi, (x - hi.astype(F32)).astype(BF16)


def kernel(
    x_hbm, cells_hbm, count_ref, value_hbm, noise_hbm, var_hbm, out_ref,
    x_ref, cells_ref, value_ref, noise_ref, var_ref,
    S, SEC, C, GR, OWNP, GC, META, PK, TC, TE, OH, OBS, RC, RE, EF,
    in_sem, row_send, row_recv, col_send, col_recv, meta_send, meta_recv, pk_send, pk_recv,
):
    n_row, n_col = lax.axis_size("row"), lax.axis_size("col")
    my_r, my_c = lax.axis_index("row"), lax.axis_index("col")
    rows, members, lanes = S.shape[1:]
    batches, slots = cells_ref.shape
    at_top, at_bottom = my_r == 0, my_r == n_row - 1
    at_left, at_right = my_c == 0, my_c == n_col - 1
    blocks = members // 8

    def present(dr, dc):
        ok = None
        for cond, d in ((my_r > 0, dr == -1), (my_r < n_row - 1, dr == 1),
                        (my_c > 0, dc == -1), (my_c < n_col - 1, dc == 1)):
            if d:
                ok = cond if ok is None else jnp.logical_and(ok, cond)
        return ok

    def device(dr, dc):
        return (jnp.clip(my_r + dr, 0, n_row - 1), jnp.clip(my_c + dc, 0, n_col - 1))

    others = [(k, dr, dc) for k, (dr, dc) in enumerate(TILES) if k != OWN]

    def mirror(k):
        dr, dc = TILES[k]
        return TILES.index((-dr, -dc))

    loads = [
        pltpu.make_async_copy(a, b, in_sem.at[i]) for i, (a, b) in enumerate((
            (x_hbm, x_ref), (cells_hbm, cells_ref), (value_hbm, value_ref),
            (noise_hbm, noise_ref), (var_hbm, var_ref)))]
    for load in loads:
        load.start()

    barrier = pltpu.get_barrier_semaphore()
    for k, dr, dc in others:
        @pl.when(present(dr, dc))
        def _(dr=dr, dc=dc):
            pl.semaphore_signal(barrier, inc=1, device_id=device(dr, dc), device_id_type=MESH)

    loads[0].wait()
    for r in (0, rows - 1) + tuple(range(1, rows - 1)):
        for f in range(3):
            S[f, r] = x_ref[f, pl.ds(r, members, stride=rows), :]

    near_r = 1 + (my_r > 0).astype(jnp.int32) + (my_r < n_row - 1).astype(jnp.int32)
    near_c = 1 + (my_c > 0).astype(jnp.int32) + (my_c < n_col - 1).astype(jnp.int32)
    pl.semaphore_wait(barrier, near_r * near_c - 1)

    def row_copies(stage, src):
        up = pltpu.make_async_remote_copy(
            src_ref=src.at[:, 0], dst_ref=GR.at[stage, 1],
            send_sem=row_send.at[stage, 0], recv_sem=row_recv.at[stage, 1],
            device_id=device(-1, 0), device_id_type=MESH)
        down = pltpu.make_async_remote_copy(
            src_ref=src.at[:, rows - 1], dst_ref=GR.at[stage, 0],
            send_sem=row_send.at[stage, 1], recv_sem=row_recv.at[stage, 0],
            device_id=device(1, 0), device_id_type=MESH)
        return up, down

    def row_start(stage, src):
        up, down = row_copies(stage, src)
        pl.when(my_r > 0)(up.start)
        pl.when(my_r < n_row - 1)(down.start)
        for side, r, wall in ((0, 0, at_top), (1, rows - 1, at_bottom)):
            @pl.when(wall)
            def _(side=side, r=r):
                GR[stage, side, 0] = src[0, r]
                GR[stage, side, 1] = src[1, r]
                GR[stage, side, 2] = -src[2, r]

    def row_wait(stage, src):
        up, down = row_copies(stage, src)

        @pl.when(my_r > 0)
        def _():
            up.wait_send()
            down_like = pltpu.make_async_remote_copy(
                src_ref=src.at[:, rows - 1], dst_ref=GR.at[stage, 0],
                send_sem=row_send.at[stage, 1], recv_sem=row_recv.at[stage, 0],
                device_id=device(-1, 0), device_id_type=MESH)
            down_like.wait_recv()

        @pl.when(my_r < n_row - 1)
        def _():
            down.wait_send()
            up_like = pltpu.make_async_remote_copy(
                src_ref=src.at[:, 0], dst_ref=GR.at[stage, 1],
                send_sem=row_send.at[stage, 0], recv_sem=row_recv.at[stage, 1],
                device_id=device(1, 0), device_id_type=MESH)
            up_like.wait_recv()

    def col_copies(stage):
        left = pltpu.make_async_remote_copy(
            src_ref=OWNP.at[stage], dst_ref=GC.at[stage, 1],
            send_sem=col_send.at[stage, 0], recv_sem=col_recv.at[stage, 1],
            device_id=device(0, -1), device_id_type=MESH)
        right = pltpu.make_async_remote_copy(
            src_ref=OWNP.at[stage], dst_ref=GC.at[stage, 0],
            send_sem=col_send.at[stage, 1], recv_sem=col_recv.at[stage, 0],
            device_id=device(0, 1), device_id_type=MESH)
        return left, right

    lane8 = lax.broadcasted_iota(jnp.int32, (8, lanes), 1)
    lane32 = lax.broadcasted_iota(jnp.int32, (32, lanes), 1)
    lane64 = lax.broadcasted_iota(jnp.int32, (members, lanes), 1)

    def col_start(stage, src):
        def pack(i, carry):
            m = pl.ds(pl.multiple_of(i * 32, 8), 32)
            packed = jnp.zeros((32, lanes), F32)
            for f in range(3):
                for r in range(rows):
                    k = f * rows + r
                    rolled = pltpu.roll(src[f, r, m, :], 2 * k + 1, 1)
                    packed = jnp.where(lane32 // 2 == k, rolled, packed)
            OWNP[stage, m, :] = packed
            return carry

        lax.fori_loop(0, members // 32, pack, 0)
        left, right = col_copies(stage)
        pl.when(my_c > 0)(left.start)
        pl.when(my_c < n_col - 1)(right.start)
        flip = jnp.where((lane64 >= 2 * rows) & (lane64 < 4 * rows), -1.0, 1.0)

        @pl.when(at_left)
        def _():
            GC[stage, 0] = pltpu.roll(OWNP[stage], lanes - 1, 1) * flip

        @pl.when(at_right)
        def _():
            GC[stage, 1] = pltpu.roll(OWNP[stage], 1, 1) * flip

    def col_wait(stage):
        left, right = col_copies(stage)

        @pl.when(my_c > 0)
        def _():
            left.wait_send()
            right.wait_recv()

        @pl.when(my_c < n_col - 1)
        def _():
            right.wait_send()
            left.wait_recv()

    def edge_flux(stage):
        even = lax.broadcasted_iota(jnp.int32, (32, lanes), 1) % 2 == 0

        def body(i, carry):
            m = pl.ds(pl.multiple_of(i * 32, 8), 32)
            own = OWNP[stage, m, :]
            lo = jnp.where(even, own, pltpu.roll(GC[stage, 0, m, :], 1, 1))
            up = jnp.where(even, pltpu.roll(GC[stage, 1, m, :], lanes - 1, 1), own)

            def unpack(v):
                h, n, t = v, pltpu.roll(v, lanes - 2 * rows, 1), pltpu.roll(v, lanes - 4 * rows, 1)
                rs = lax.rsqrt(h)
                return cell(h, n, t, n * (rs * rs), ROOT_G * (h * rs))

            done = face(unpack(lo), unpack(up))
            for f in range(3):
                EF[f, m, :] = done[f]
            return carry

        lax.fori_loop(0, members // 32, body, 0)

    def advance(stage, src, tall, spans, finish):
        lane_b = lax.broadcasted_iota(jnp.int32, (tall, lanes), 1)

        def body(i, carry):
            m = pl.ds(pl.multiple_of(i * tall, 8), tall)
            edge = [EF[f, m, :] for f in range(3)]

            def load(r):
                if r < 0:
                    f = [GR[stage, 0, f, m, :] for f in range(3)]
                elif r >= rows:
                    f = [GR[stage, 1, f, m, :] for f in range(3)]
                else:
                    f = [src[f, r, m, :] for f in range(3)]
                return f

            def derive(f):
                rs = lax.rsqrt(f[0])
                rec = rs * rs
                return f[1] * rec, f[2] * rec, ROOT_G * (f[0] * rs)

            def rowcell(f, d):
                return cell(f[0], f[2], f[1], d[1], d[2])

            for first, last in spans:
                fc = load(first)
                dc = derive(fc)
                below = None
                for r in range(first, last):
                    fn = dn = above = None
                    if r + 1 < last:
                        fn = load(r + 1)
                        dn = derive(fn)
                        above = face(rowcell(fc, dc), rowcell(fn, dn))
                    left = [pltpu.roll(v, 1, 1) for v in (*fc, dc[0], dc[2])]
                    flux = face(cell(*left), cell(*fc, dc[0], dc[2]))
                    out = []
                    for f, g in ((0, 0), (1, 2), (2, 1)):
                        q = pltpu.roll(edge[f], lanes - 1 - 2 * r, 1)
                        low = jnp.where(lane_b == 0, q, flux[f])
                        high = jnp.where(lane_b == lanes - 1, q, pltpu.roll(low, lanes - 1, 1))
                        gain = high - low
                        if above is not None:
                            gain = gain + above[g]
                        if below is not None:
                            gain = gain - below[g]
                        out.append(gain * (-1.0 / SPACING))
                    finish(r, m, fc, out)
                    fc, dc, below = fn, dn, above
            return carry

        lax.fori_loop(0, members // tall, body, 0)

    def outer(stage, src, target, factor):
        def body(i, carry):
            m = pl.ds(pl.multiple_of(i * OUTER, 8), OUTER)

            def rowcell(h, n, t):
                rs = lax.rsqrt(h)
                return cell(h, t, n, t * (rs * rs), ROOT_G * (h * rs))

            for side, r, sign in ((0, 0, 1.0), (1, rows - 1, -1.0)):
                ghost = rowcell(*(GR[stage, side, f, m, :] for f in range(3)))
                inside = rowcell(*(src[f, r, m, :] for f in range(3)))
                flux = face(ghost, inside) if side == 0 else face(inside, ghost)
                for f, g in ((0, 0), (1, 2), (2, 1)):
                    target[f, r, m, :] = target[f, r, m, :] + flux[g] * (sign * factor / SPACING)
            return carry

        lax.fori_loop(0, members // OUTER, body, 0)

    def finish1(r, m, fields, tend):
        for f in range(3):
            SEC[f, r, m, :] = fields[f] + STEP * tend[f]

    def finish2(r, m, fields, tend):
        for f in range(3):
            C[f, r, m, :] = 0.5 * (S[f, r, m, :] + fields[f] + STEP * tend[f])

    row_start(0, S)
    for load in loads[1:]:
        load.wait()
    META[OWN] = jnp.zeros((8, lanes), F32)
    META[OWN, 0:batches, 0:slots] = cells_ref[...].astype(F32)
    col_start(0, S)

    def meta_copy(k, dr, dc):
        return pltpu.make_async_remote_copy(
            src_ref=META.at[OWN], dst_ref=META.at[mirror(k)],
            send_sem=meta_send.at[k], recv_sem=meta_recv.at[mirror(k)],
            device_id=device(dr, dc), device_id_type=MESH)

    def pk_copy(b, k, dr, dc):
        return pltpu.make_async_remote_copy(
            src_ref=PK.at[b, OWN], dst_ref=PK.at[b, mirror(k)],
            send_sem=pk_send.at[b, k], recv_sem=pk_recv.at[b, mirror(k)],
            device_id=device(dr, dc), device_id_type=MESH)

    for k, dr, dc in others:
        @pl.when(present(dr, dc))
        def _(k=k, dr=dr, dc=dc):
            meta_copy(k, dr, dc).start()

        @pl.when(jnp.logical_not(present(dr, dc)))
        def _(k=k):
            META[k] = jnp.zeros((8, lanes), F32)
            for b in range(batches):
                PK[b, k] = jnp.zeros((slots, lanes), F32)

    eye = lax.broadcasted_iota(jnp.int32, (slots, lanes), 0) == lax.broadcasted_iota(
        jnp.int32, (slots, lanes), 1)

    def column(row):
        return jnp.sum(jnp.where(eye, row, 0.0), axis=1, keepdims=True)

    lane_s = lax.broadcasted_iota(jnp.int32, (slots, lanes), 1).astype(F32)
    wide = lambda row: jnp.concatenate([row, jnp.zeros((1, lanes - slots), F32)], axis=1)
    for b in range(batches):
        own_cell = column(META[OWN, b:b + 1, :])
        for r in range(rows):
            OH[b, :, r * lanes:(r + 1) * lanes] = jnp.where(
                own_cell == lane_s + float(r * lanes), 1.0, 0.0).astype(BF16)
        OBS[b, 0] = jnp.broadcast_to(column(wide(value_ref[b:b + 1, :])), (slots, lanes))
        OBS[b, 1] = jnp.broadcast_to(column(wide(var_ref[b:b + 1, :])), (slots, lanes))

    col_wait(0)
    edge_flux(0)
    advance(0, S, INNER, ((0, rows),), finish1)
    row_wait(0, S)
    outer(0, S, SEC, STEP)

    row_start(1, SEC)
    col_start(1, SEC)

    for k, dr, dc in others:
        @pl.when(present(dr, dc))
        def _(k=k, dr=dr, dc=dc):
            meta_copy(k, dr, dc).wait_send()
            meta_copy(mirror(k), -dr, -dc).wait_recv()

    window = 2 * LOC
    members_1 = float(members - 1)
    lane_1 = lax.broadcasted_iota(jnp.int32, (1, lanes), 1)
    in_window = lane_1 % window
    edge_row = (lane_1 // window).astype(F32)
    edge_col = jnp.where(in_window < LOC, lanes - LOC + in_window, in_window - LOC).astype(F32)
    inv_loc = 1.0 / (LOC * LOC)
    for b in range(batches):
        for k, (dr, dc) in enumerate(TILES):
            at = column(META[k, b:b + 1, :])
            g_row = jnp.floor(at * (1.0 / lanes))
            g_col = at - g_row * lanes + float(dc * lanes)
            g_row = g_row + float(dr * rows)
            where = pl.ds((k % 3) * slots, slots)
            if dc == 0:
                dcol = lane_s - g_col
                dcol = dcol * dcol
                for r in range(rows):
                    drow = float(r) - g_row
                    t = jnp.maximum(1.0 - (dcol + drow * drow) * inv_loc, 0.0)
                    TC[b, where, r * lanes:(r + 1) * lanes] = t * t * (1.0 / members_1)
            else:
                dcol = edge_col - g_col
                drow = edge_row - g_row
                t = jnp.maximum(1.0 - (dcol * dcol + drow * drow) * inv_loc, 0.0)
                TE[b, (k - 3) * slots:(k - 2) * slots, :] = t * t * (1.0 / members_1)

    col_wait(1)
    edge_flux(1)
    advance(1, SEC, INNER, ((0, rows),), finish2)
    row_wait(1, SEC)
    outer(1, SEC, C, 0.5 * STEP)

    dot = functools.partial(lax.dot_general, preferred_element_type=F32)
    nn = (((1,), (0,)), ((), ()))
    nt = (((1,), (1,)), ((), ()))

    def operands(packets):
        lane = lax.broadcasted_iota(jnp.int32, packets.shape, 1)
        swapped = pltpu.roll(packets, lanes // 2, 1)
        anom = jnp.where(lane < members, packets, swapped)
        weight = jnp.where(lane < members, swapped, packets)
        hi, lo = split2(anom)
        w_hi = weight.astype(BF16).astype(F32)
        w = jnp.where(lane < members, w_hi, weight - w_hi)
        return (jnp.concatenate([hi, lo], axis=1),
                jnp.concatenate([w, w], axis=0).T.astype(BF16))

    def increment(anom, weight, centred, taper):
        cov = dot(anom, centred, nn) * taper
        hi, lo = split2(cov)
        both = dot(weight, jnp.concatenate([hi, lo], axis=0), nn)
        return both[:members] + both[members:]

    def centre(v):
        hi, lo = split2(v - jnp.mean(v, axis=0, keepdims=True))
        return jnp.concatenate([hi, lo, hi, lo], axis=0)

    for b in range(batches):
        depth = jnp.concatenate([C[0, r] for r in range(rows)], axis=1)
        hi, rest = depth.astype(BF16), None
        rest = depth - hi.astype(F32)
        mid, low = split2(rest)
        onehot = OH[b]
        prior = dot(onehot, hi, nt) + (dot(onehot, mid, nt) + dot(onehot, low, nt))
        anom = prior - jnp.mean(prior, axis=1, keepdims=True)
        spread = jnp.sum(anom * anom, axis=1, keepdims=True) * (1.0 / members_1)
        slot = lax.broadcasted_iota(jnp.int32, (slots, members), 0)
        live = jnp.where(slot < count_ref[0, 0, b], 1.0, 0.0)
        weight = live * (OBS[b, 0, :, :members] + noise_ref[b] - prior) / (
            spread + OBS[b, 1, :, :members])
        PK[b, OWN] = jnp.concatenate([anom, weight], axis=1)
        for k, dr, dc in others:
            @pl.when(present(dr, dc))
            def _(k=k, dr=dr, dc=dc):
                pk_copy(b, k, dr, dc).start()

        def prepare(f, carry):
            edges = jnp.zeros((members, lanes), F32)
            for r in range(rows):
                rolled = pltpu.roll(C[f, r], window * r + LOC, 1)
                edges = jnp.where(lane64 // window == r, rolled, edges)
            RE[f] = centre(edges)
            for pair in range(rows // 2):
                v = jnp.concatenate([C[f, 2 * pair], C[f, 2 * pair + 1]], axis=1)
                RC[f, pair] = centre(v)
            return carry

        for f in range(3):
            prepare(f, 0)

        def arrive(ks):
            for k, dr, dc in others:
                if k in ks:
                    @pl.when(present(dr, dc))
                    def _(k=k, dr=dr, dc=dc):
                        pk_copy(b, k, dr, dc).wait_send()
                        pk_copy(b, mirror(k), -dr, -dc).wait_recv()

        def update(f, anom_c, weight_c, taper):
            for pair in range(rows // 2):
                span = slice(2 * pair * lanes, (2 * pair + 2) * lanes)
                inc = increment(anom_c, weight_c, RC[f, pair], taper(span))
                C[f, 2 * pair] = C[f, 2 * pair] + inc[:, :lanes]
                C[f, 2 * pair + 1] = C[f, 2 * pair + 1] + inc[:, lanes:]

        here = operands(PK[b, OWN])
        for f in range(3):
            update(f, *here, lambda span: TC[b, slots:2 * slots, span])
        arrive((0, 2))
        beside = operands(jnp.concatenate([PK[b, 0], PK[b, 2]], axis=0))
        for f in range(3):
            update(f, *beside, lambda span: jnp.concatenate(
                [TC[b, :slots, span], TC[b, 2 * slots:, span]], axis=0))
        arrive((3, 4, 5, 6, 7, 8))
        anom_e, weight_e = operands(PK[b, 3:9].reshape(6 * slots, lanes))

        def update_edges(f, carry):
            inc = increment(anom_e, weight_e, RE[f], TE[b])
            outer = (lane64 < LOC) | (lane64 >= lanes - LOC)
            for r in range(rows):
                back = pltpu.roll(inc, (lanes - (window * r + LOC)) % lanes, 1)
                done = C[f, r] + jnp.where(outer, back, 0.0)
                if b < batches - 1:
                    C[f, r] = done
                else:
                    out_ref[f, pl.ds(r, members, stride=rows), :] = done
            return carry

        for f in range(3):
            update_edges(f, 0)


def body(state, gauge_cells, gauge_count, obs_value, obs_noise, obs_var):
    fields, members, rows, lanes = state.shape
    batches, slots = gauge_cells.shape[2:]
    vmem = pl.BlockSpec(memory_space=pltpu.VMEM)
    hbm = pl.BlockSpec(memory_space=pltpu.HBM)
    dma = pltpu.SemaphoreType.DMA
    grid = (fields, rows, members, lanes)
    out = pl.pallas_call(
        kernel,
        out_shape=jax.ShapeDtypeStruct((fields, members * rows, lanes), F32),
        in_specs=[hbm, hbm, pl.BlockSpec(memory_space=pltpu.SMEM), hbm, hbm, hbm],
        out_specs=vmem,
        scratch_shapes=[
            pltpu.VMEM((fields, members * rows, lanes), F32),
            pltpu.VMEM((batches, slots), gauge_cells.dtype),
            pltpu.VMEM((batches, slots), F32),
            pltpu.VMEM((batches, slots, members), F32),
            pltpu.VMEM((batches, slots), F32),
            pltpu.VMEM(grid, F32),
            pltpu.VMEM(grid, F32),
            pltpu.VMEM(grid, F32),
            pltpu.VMEM((2, 2, fields, members, lanes), F32),
            pltpu.VMEM((2, members, lanes), F32),
            pltpu.VMEM((2, 2, members, lanes), F32),
            pltpu.VMEM((9, 8, lanes), F32),
            pltpu.VMEM((batches, 9, slots, lanes), F32),
            pltpu.VMEM((batches, 3 * slots, rows * lanes), F32),
            pltpu.VMEM((batches, 6 * slots, lanes), F32),
            pltpu.VMEM((batches, slots, rows * lanes), BF16),
            pltpu.VMEM((batches, 2, slots, lanes), F32),
            pltpu.VMEM((fields, rows // 2, 4 * members, 2 * lanes), BF16),
            pltpu.VMEM((fields, 4 * members, lanes), BF16),
            pltpu.VMEM((fields, members, lanes), F32),
            dma((5,)),
            dma((2, 2)), dma((2, 2)), dma((2, 2)), dma((2, 2)),
            dma((9,)), dma((9,)), dma((batches, 9)), dma((batches, 9)),
        ],
        compiler_params=pltpu.CompilerParams(
            collective_id=0, has_side_effects=True, vmem_limit_bytes=62 * 1024 * 1024),
    )(
        state.reshape(fields, members * rows, lanes),
        gauge_cells.reshape(batches, slots),
        gauge_count,
        obs_value.reshape(batches, slots),
        obs_noise.reshape(batches, slots, members),
        obs_var.reshape(batches, slots),
    )
    return out.reshape(state.shape)


def solution(mesh):
    placed = (
        P(None, None, "row", "col"),
        P("row", "col", None, None),
        P("row", "col", None),
        P("row", "col", None, None),
        P("row", "col", None, None, None),
        P("row", "col", None, None),
    )
    return jax.shard_map(
        body, mesh=mesh, in_specs=placed, out_specs=P(None, None, "row", "col"), check_vma=False
    )
```
